256 devices in a mesh: seq: 64 (over y, z, core), fsdp: 4 (over x).
Axes of the slice: x: 4, y: 4, z: 8, core: 2. Of those that a mesh axis runs over, the one named last changes fastest.
Arguments:
- tokens: bfloat16 [65536, 4096], P('seq', 'fsdp'), may hold values from -6 to 6
- projection: bfloat16 [3, 4096, 2048], P(None, 'seq', 'fsdp'), may hold values from -0.09375 to 0.09375
- log_decay: float32 [65536, 16], P('seq', 'fsdp'), may hold values from -2 to 0, as said below
Outputs:
- attended: bfloat16 [65536, 2048], P('seq', 'fsdp')
The draws below stay inside these ranges and needn't reach their ends.
Inputs may be any that keep to these rules, and one draw needn't show every extreme that they name: `log_decay`: negative logarithms of decay factors, one for each position and head.
All inputs are finite; a program needn't handle non-finite values.
Results may differ from the reference program's by a relative error of at most 0.006.
Values may be sent and summed in bfloat16 or wider, within the bound.
No kernel may reach another device: no remote copies, remote signals or barrier semaphores. Data moves between devices by JAX's collectives and lax.ppermute only.
A program may use at most 64 MiB of HBM per device.

```python
import math
import jax
import jax.numpy as jnp
from jax import lax

D = 4096
ATTENDING_GROUPS = 16
HEAD = 128
BLK = 512
TOK_DEV = 1024
TOKENS = 65536


def draw_log_decay(key, part):
    key = jax.random.fold_in(key, 11)
    lookup_vectors = jax.random.split(key, 9)
    fast_count = max(1, ATTENDING_GROUPS // 5)
    medium_count = max(1, ATTENDING_GROUPS // 2 - fast_count)
    offset_scaling = jnp.exp(jnp.clip(jax.random.normal(lookup_vectors[3], (TOKENS, ATTENDING_GROUPS), jnp.float32) * 0.35, -math.log(2.0), math.log(2.0)))
    ranks = jax.random.permutation(lookup_vectors[0], ATTENDING_GROUPS)
    fast = ranks < fast_count
    medium = (ranks >= fast_count) & (ranks < fast_count + medium_count)
    slow_rate = jnp.exp(jax.random.uniform(lookup_vectors[1], (ATTENDING_GROUPS,), jnp.float32, math.log(0.3), math.log(0.9))) / TOKENS
    medium_rate = jnp.exp(jax.random.uniform(lookup_vectors[7], (ATTENDING_GROUPS,), jnp.float32, math.log(0.25), math.log(4.0))) / TOK_DEV
    fast_rate = jnp.exp(jax.random.uniform(lookup_vectors[2], (ATTENDING_GROUPS,), jnp.float32, math.log(1.0 / 50.0), math.log(1.0 / 30.0)))
    default_fading_speed = jnp.where(fast, fast_rate, jnp.where(medium, medium_rate, slow_rate))
    segment_len = max(TOKENS // 64, 1)
    segment_factor = jnp.exp(jax.random.uniform(lookup_vectors[4], (64 + 1, ATTENDING_GROUPS), jnp.float32, -math.log(2.0), math.log(2.0)))
    segment_index = jnp.minimum(jnp.arange(TOKENS) // segment_len, 64)
    stretch_speeds = segment_factor[segment_index]
    leading_spot = jax.random.randint(lookup_vectors[5], (ATTENDING_GROUPS,), 0, TOKENS)
    trailing_spot = (leading_spot + jax.random.randint(lookup_vectors[8], (ATTENDING_GROUPS,), 1, TOKENS)) % TOKENS
    spike_offsets = jnp.stack([leading_spot, trailing_spot])
    spike_strength = jax.random.uniform(lookup_vectors[6], (2, ATTENDING_GROUPS), jnp.float32, 0.6, 0.8)
    sequence_offsets = jnp.arange(TOKENS)[:, None, None]
    sudden_spike_list = jnp.sum(jnp.where(sequence_offsets == spike_offsets[None], jnp.log(spike_strength)[None], 0.0), axis=1)
    return (-default_fading_speed[None, :] * offset_scaling * stretch_speeds + sudden_spike_list).astype(jnp.float32)


def block_levels(stream_key, extent, pieces, low, high):
    loudness, own = 1.0, jax.random.fold_in(stream_key, 6)
    for axis_at, parts in pieces:
        steps = jnp.exp(jax.random.uniform(jax.random.fold_in(own, axis_at), (parts,), jnp.float32, low / len(pieces), high / len(pieces)))
        loudness = loudness * jnp.repeat(steps, extent[axis_at] // parts).reshape([-1 if axis == axis_at else 1 for axis in range(len(extent))])
    return loudness


def scatter_about(rng, extent, deviation, limit, cuts=(), dtype=jnp.bfloat16):
    level = block_levels(rng, extent, cuts, -0.22, 0.18) if cuts else 1.0
    entries = jax.random.normal(rng, extent, jnp.float32) * deviation * level
    return jnp.minimum(jnp.maximum(entries, -limit), limit).astype(dtype)


def setup_inputs(seed: int = 0) -> dict:
    splits = jax.random.split(jax.random.key(seed), 4)
    return {
        "tokens": scatter_about(splits[0], (TOKENS, D), 1.0, 6.0, ((0, 64), (1, 4))),
        "projection": scatter_about(splits[1], (3, D, ATTENDING_GROUPS * HEAD), D ** -0.5, 0.09375, ((1, 64), (2, 4))),
        "log_decay": draw_log_decay(jax.random.fold_in(splits[3], 71), 0),
    }


def block_attention(state, inputs):
    queries, key_vecs, value_vecs, decay = inputs
    running = jnp.cumsum(decay, axis=0)
    across = running.T
    gap = across[:, :, None] - across[:, None, :]
    lower = jnp.arange(gap.shape[1])[:, None] >= jnp.arange(gap.shape[2])[None, :]
    fading = jnp.exp(jnp.where(lower[None], gap, -1e+30))
    scores = jnp.einsum('thd,shd->hts', queries.astype(jnp.float32), key_vecs.astype(jnp.float32), precision=lax.Precision.HIGHEST)
    weights = (fading * scores).astype(jnp.bfloat16)
    intra = jnp.einsum('hts,she->the', weights.astype(jnp.float32), value_vecs.astype(jnp.float32), precision=lax.Precision.HIGHEST)
    inter = jnp.exp(running)[:, :, None] * jnp.einsum('thd,hde->the', queries.astype(jnp.float32), state, precision=lax.Precision.HIGHEST)
    last = running[-1]
    carried = key_vecs.astype(jnp.float32) * jnp.exp(last[None, :] - running)[:, :, None]
    fresh = jnp.einsum('shd,she->hde', carried, value_vecs.astype(jnp.float32), precision=lax.Precision.HIGHEST)
    new_state = jnp.exp(last)[:, None, None] * state + fresh
    mixed = intra + inter
    normed = mixed * lax.rsqrt(lax.optimization_barrier(jnp.mean(mixed * mixed, axis=-1, keepdims=True)) + 1e-06)
    return (new_state, normed.astype(jnp.bfloat16))

def reference(tokens, projection, log_decay):
    block_count = TOKENS // BLK
    query_raw = jnp.dot(tokens, projection[0], preferred_element_type=jnp.float32)
    key_raw = jnp.dot(tokens, projection[1], preferred_element_type=jnp.float32)
    value_raw = jnp.dot(tokens, projection[2], preferred_element_type=jnp.float32)
    queries = jax.nn.silu(query_raw).astype(jnp.bfloat16).reshape(block_count, BLK, ATTENDING_GROUPS, HEAD)
    key_vecs = jax.nn.silu(key_raw).astype(jnp.bfloat16).reshape(block_count, BLK, ATTENDING_GROUPS, HEAD)
    value_vecs = value_raw.astype(jnp.bfloat16).reshape(block_count, BLK, ATTENDING_GROUPS, HEAD)
    decay = log_decay.reshape(block_count, BLK, ATTENDING_GROUPS)
    start = jnp.zeros((ATTENDING_GROUPS, HEAD, HEAD), jnp.float32)
    final, outputs = lax.scan(block_attention, start, (queries, key_vecs, value_vecs, decay))
    return outputs.reshape(TOKENS, ATTENDING_GROUPS * HEAD)
```

```python
import functools

import jax
import jax.numpy as jnp
from jax import lax
from jax.experimental import pallas as pl
from jax.experimental.pallas import tpu as pltpu
from jax.sharding import PartitionSpec as P

BLK = 512
HEAD = 128
F32 = jnp.float32
BF16 = jnp.bfloat16
EXACT = lax.Precision.HIGHEST
VMEM_LIMIT = 56 * 2**20


def silu(v):
    return v / (1.0 + jnp.exp(-v))


def project(step, tokens, weights, acc):
    for d in range(4):

        @pl.when(step == d)
        def _(d=d):
            for c in range(weights.shape[0]):
                part = jnp.dot(tokens[d][...], weights[c], preferred_element_type=F32)
                acc[c] = part if d == 0 else acc[c] + part


def kv_kernel(order, own, left, right, far, weights, run, last, k_out, v_out, fresh, acc):
    step = pl.program_id(0)
    project(step, (own, left, right, far), weights, acc)

    @pl.when(step == 3)
    def _():
        for h in range(4):
            cols = slice(h * HEAD, (h + 1) * HEAD)
            k = silu(acc[0, :, cols]).astype(BF16)
            v = acc[1, :, cols].astype(BF16)
            k_out[:, cols] = k
            v_out[:, cols] = v
            fade = jnp.exp(last[:, h : h + 1] - run[:, h : h + 1])
            carried = (k.astype(F32) * fade).astype(BF16)
            fresh[h] = lax.dot_general(
                carried, v, (((0,), (0,)), ((), ())), preferred_element_type=F32
            )


def q_kernel(order, own, left, right, far, weights, run, across, k, v, q_out, intra, acc):
    step = pl.program_id(0)
    project(step, (own, left, right, far), weights, acc)

    @pl.when(step == 3)
    def _():
        half = BLK // 2
        for h in range(4):
            cols = slice(h * HEAD, (h + 1) * HEAD)
            q = silu(acc[0, :, cols]).astype(BF16)
            q_out[:, cols] = q
            for t in range(2):
                rows = slice(t * half, (t + 1) * half)
                wide = (t + 1) * half
                scores = lax.dot_general(
                    q[rows],
                    k[:wide, cols],
                    (((1,), (1,)), ((), ())),
                    preferred_element_type=F32,
                )
                gap = run[rows, h : h + 1] - across[h : h + 1, :wide]
                at = lax.broadcasted_iota(jnp.int32, gap.shape, 0) + t * half
                lower = at >= lax.broadcasted_iota(jnp.int32, gap.shape, 1)
                fading = jnp.exp(jnp.where(lower, gap, -1e30))
                mix = (fading * scores).astype(BF16)
                intra[rows, cols] = jnp.dot(mix, v[:wide, cols], preferred_element_type=F32)


def final_kernel(q, intra, run, state, out):
    for h in range(4):
        cols = slice(h * HEAD, (h + 1) * HEAD)
        whole = state[0, h]
        high = whole.astype(BF16)
        low = (whole - high.astype(F32)).astype(BF16)
        inter = jnp.dot(q[:, cols], high, preferred_element_type=F32)
        inter += jnp.dot(q[:, cols], low, preferred_element_type=F32)
        mixed = intra[:, cols] + jnp.exp(run[:, h : h + 1]) * inter
        scale = lax.rsqrt(jnp.mean(mixed * mixed, axis=-1, keepdims=True) + 1e-06)
        out[:, cols] = (mixed * scale).astype(BF16)


def params():
    return pltpu.CompilerParams(
        dimension_semantics=("arbitrary",), vmem_limit_bytes=VMEM_LIMIT
    )


def token_specs(block):
    spec = pl.BlockSpec((BLK, 1024), lambda d, order: (block, 0))
    return [spec, spec, spec, pl.BlockSpec((BLK, 1024), lambda d, order: (0, 0))]


def fixed(shape):
    return pl.BlockSpec(shape, lambda d, order: (0,) * len(shape))


def project_kv(block, order, tokens, weights, run, last):
    width = weights.shape[2]
    return pl.pallas_call(
        kv_kernel,
        grid_spec=pltpu.PrefetchScalarGridSpec(
            num_scalar_prefetch=1,
            grid=(4,),
            in_specs=[
                *token_specs(block),
                pl.BlockSpec((2, 1024, width), lambda d, order: (0, order[d], 0)),
                fixed((BLK, 4)),
                fixed((1, 4)),
            ],
            out_specs=[fixed((BLK, width)), fixed((BLK, width)), fixed((4, HEAD, HEAD))],
            scratch_shapes=[pltpu.VMEM((2, BLK, width), F32)],
        ),
        out_shape=[
            jax.ShapeDtypeStruct((BLK, width), BF16),
            jax.ShapeDtypeStruct((BLK, width), BF16),
            jax.ShapeDtypeStruct((4, HEAD, HEAD), F32),
        ],
        compiler_params=params(),
        cost_estimate=pl.CostEstimate(
            flops=2 * BLK * 4096 * 1024, bytes_accessed=14 * 2**20, transcendentals=BLK * 512
        ),
        name=f"kv{block}",
    )(order, *tokens, weights, run, last)


def project_q(block, order, tokens, weights, run, across, k, v):
    width = weights.shape[2]
    return pl.pallas_call(
        q_kernel,
        grid_spec=pltpu.PrefetchScalarGridSpec(
            num_scalar_prefetch=1,
            grid=(4,),
            in_specs=[
                *token_specs(block),
                pl.BlockSpec((1, 1024, width), lambda d, order: (0, order[d], 0)),
                fixed((BLK, 4)),
                fixed((4, BLK)),
                fixed((BLK, width)),
                fixed((BLK, width)),
            ],
            out_specs=[fixed((BLK, width)), fixed((BLK, width))],
            scratch_shapes=[pltpu.VMEM((1, BLK, width), F32)],
        ),
        out_shape=[
            jax.ShapeDtypeStruct((BLK, width), BF16),
            jax.ShapeDtypeStruct((BLK, width), F32),
        ],
        compiler_params=params(),
        cost_estimate=pl.CostEstimate(
            flops=2 * BLK * 4096 * 512, bytes_accessed=10 * 2**20, transcendentals=BLK * BLK * 4
        ),
        name=f"q{block}",
    )(order, *tokens, weights, run, across, k, v)


def finish(q, intra, run, states):
    width = q[0].shape[1]
    rows = 2 * BLK

    def body(q0, q1, i0, i1, run, state, out):
        for b, (qb, ib) in enumerate(((q0, i0), (q1, i1))):

            @pl.when(pl.program_id(0) == b)
            def _(qb=qb, ib=ib):
                final_kernel(qb, ib, run, state, out)

    whole = pl.BlockSpec((BLK, width), lambda b: (0, 0))
    return pl.pallas_call(
        body,
        grid=(2,),
        in_specs=[
            whole,
            whole,
            whole,
            whole,
            pl.BlockSpec((BLK, 4), lambda b: (b, 0)),
            pl.BlockSpec((1, 4, HEAD, HEAD), lambda b: (b, 0, 0, 0)),
        ],
        out_specs=pl.BlockSpec((BLK, width), lambda b: (b, 0)),
        out_shape=jax.ShapeDtypeStruct((rows, width), BF16),
        compiler_params=params(),
        cost_estimate=pl.CostEstimate(
            flops=4 * rows * width * HEAD, bytes_accessed=5 * 2**20, transcendentals=rows * 8
        ),
        name="finish",
    )(*q, *intra, run, states)


def ring(n, by):
    return [(i, (i + by) % n) for i in range(n)]


def gather_tokens(tokens):
    n = lax.axis_size("fsdp")
    ahead = functools.partial(lax.ppermute, axis_name="fsdp", perm=ring(n, 1))
    back = functools.partial(lax.ppermute, axis_name="fsdp", perm=ring(n, -1))
    top, bottom = tokens[:BLK], tokens[BLK:]
    left0, right1 = ahead(top), back(bottom)
    left1, right0 = ahead(bottom), back(top)
    far0, far1 = ahead(left0), back(right1)
    return (top, left0, right0, far0), (bottom, left1, right1, far1)


def entering(state, whole):
    n = lax.axis_size("seq")
    place = lax.axis_index("seq")
    heads = whole.shape[1]
    at = jnp.arange(n)
    between = (at[None, None, :] > at[None, :, None]) & (at[None, None, :] < at[:, None, None])
    head = place * heads // n
    mine = lax.dynamic_index_in_dim(whole, head, 1, False)
    gap = jnp.sum(jnp.where(between, mine[None, None, :], 0.0), axis=2)
    factor = jnp.where(at[:, None] > at[None, :], jnp.exp(gap), 0.0)
    piece = lax.all_to_all(state.reshape(n, -1, HEAD), "seq", 0, 0, tiled=True)
    prefix = jnp.dot(factor, piece.reshape(n, -1), precision=EXACT)
    back = lax.all_to_all(prefix.reshape(piece.shape), "seq", 0, 0, tiled=True)
    return back.reshape(state.shape)


def on_device(tokens, projection, log_decay):
    heads = log_decay.shape[1]
    x = lax.axis_index("fsdp")
    order = jnp.remainder(x + jnp.array([0, 3, 1, 2], jnp.int32), 4).astype(jnp.int32)
    first, second = gather_tokens(tokens)
    kv_weights = lax.all_gather(projection[1:], "seq", axis=1, tiled=True)
    q_weights = lax.all_gather(projection[:1], "seq", axis=1, tiled=True)

    decay = log_decay.reshape(2, BLK, heads)
    lower = (jnp.arange(BLK)[:, None] >= jnp.arange(BLK)[None, :]).astype(F32)
    run = jnp.einsum("ts,bsh->bth", lower, decay, precision=EXACT)
    across = run.transpose(0, 2, 1)
    last = run[:, -1]
    whole = lax.all_gather(last[0] + last[1], "seq")

    k0, v0, fresh0 = project_kv(0, order, first, kv_weights, run[0], last[:1])
    k1, v1, fresh1 = project_kv(0, order, second, kv_weights, run[1], last[1:])
    kept = jnp.exp(last[1])[:, None, None]
    entry = entering(kept * fresh0 + fresh1, whole)
    q0, intra0 = project_q(0, order, first, q_weights, run[0], across[0], k0, v0)
    q1, intra1 = project_q(0, order, second, q_weights, run[1], across[1], k1, v1)
    states = jnp.stack([entry, jnp.exp(last[0])[:, None, None] * entry + fresh0])
    return finish((q0, q1), (intra0, intra1), run.reshape(2 * BLK, heads), states)


def solution(mesh):
    in_specs = (P("seq", "fsdp"), P(None, "seq", "fsdp"), P("seq", "fsdp"))
    out_specs = P("seq", "fsdp")
    return jax.shard_map(
        on_device, mesh=mesh, in_specs=in_specs, out_specs=out_specs, check_vma=False
    )
```

```python
import functools

import jax
import jax.numpy as jnp
from jax import lax
from jax.experimental import pallas as pl
from jax.experimental.pallas import tpu as pltpu
from jax.sharding import PartitionSpec as P

BLK = 512
HEAD = 128
DEPTH = 1024
X = 4
MIB = 2**20
F32 = jnp.float32
BF16 = jnp.bfloat16
EXACT = lax.Precision.HIGHEST
LEFT = pl.BlockSpec(memory_space=pl.ANY)
SCALARS = pl.BlockSpec(memory_space=pltpu.SMEM)


def silu(v):
    return v / (1.0 + jnp.exp(-v))


class Operands:
    def __init__(self, order, tokens, weights, matrices, token_slots, weight_slots, sems):
        self.token_slots, self.weight_slots = token_slots, weight_slots
        own, *rest = tokens
        self.pending = {}
        count = 0

        def add(key, src, dst):
            nonlocal count
            copy = pltpu.make_async_copy(src, dst, sems.at[count])
            copy.start()
            self.pending.setdefault(key, []).append(copy)
            count += 1

        def token(b):
            for d in range(X):
                src = own.at[pl.ds(b * BLK, BLK)] if d == 0 else rest[3 * b + d - 1]
                add(("t", b), src, token_slots.at[b, :, pl.ds(d * DEPTH, DEPTH)])

        def weight(m):
            for d in range(X):
                rows = pl.ds(pl.multiple_of(order[d] * DEPTH, DEPTH), DEPTH)
                add(("w", m), weights.at[matrices[m], rows], weight_slots.at[m, pl.ds(d * DEPTH, DEPTH)])

        weight(0)
        token(0)
        for m in range(1, len(matrices)):
            weight(m)
        token(1)

    def project(self, b, m):
        for key in (("t", b), ("w", m)):
            for copy in self.pending.pop(key, ()):
                copy.wait()
        return jnp.dot(self.token_slots[b], self.weight_slots[m], preferred_element_type=F32)


def kv_kernel(order, *refs):
    tokens, weights = refs[:7], refs[7]
    run, last, k_out, v_out, fresh, final, *scratch = refs[8:]
    operands = Operands(order, tokens, weights, (1, 2), *scratch)
    for b in range(2):
        rows = slice(b * BLK, (b + 1) * BLK)
        k = silu(operands.project(b, 0)).astype(BF16)
        k_out[rows] = k
        v = operands.project(b, 1).astype(BF16)
        v_out[rows] = v
        for h in range(4):
            cols = slice(h * HEAD, (h + 1) * HEAD)
            ends = last[b : b + 1, h : h + 1]
            fade = jnp.exp(ends - run[b, :, h : h + 1])
            carried = (k[:, cols].astype(F32) * fade).astype(BF16)
            new = lax.dot_general(
                carried, v[:, cols], (((0,), (0,)), ((), ())), preferred_element_type=F32
            )
            if b == 0:
                fresh[h] = new
            else:
                final[h] = jnp.exp(ends) * fresh[h] + new


def q_kernel(order, *refs):
    tokens, weights = refs[:7], refs[7]
    run, across, k, v, q_out, intra, *scratch = refs[8:]
    operands = Operands(order, tokens, weights, (0,), *scratch)
    half = BLK // 2
    for b in range(2):
        base = b * BLK
        q = silu(operands.project(b, 0)).astype(BF16)
        q_out[base : base + BLK] = q
        for h in range(4):
            cols = slice(h * HEAD, (h + 1) * HEAD)
            for t in range(2):
                rows = slice(t * half, (t + 1) * half)
                wide = (t + 1) * half
                scores = lax.dot_general(
                    q[rows, cols],
                    k[base : base + wide, cols],
                    (((1,), (1,)), ((), ())),
                    preferred_element_type=F32,
                )
                gap = run[b, rows, h : h + 1] - across[b, h : h + 1, :wide]
                at = lax.broadcasted_iota(jnp.int32, gap.shape, 0) + t * half
                lower = at >= lax.broadcasted_iota(jnp.int32, gap.shape, 1)
                fading = jnp.exp(jnp.where(lower, gap, -1e30))
                mix = (fading * scores).astype(BF16)
                intra[base + t * half : base + wide, cols] = jnp.dot(
                    mix, v[base : base + wide, cols], preferred_element_type=F32
                )


def finish_kernel(q, intra, run, last, entry, fresh, out):
    b = pl.program_id(0)
    for h in range(4):
        cols = slice(h * HEAD, (h + 1) * HEAD)
        later = jnp.exp(last[0:1, h : h + 1]) * entry[h] + fresh[h]
        state = jnp.where(b == 0, entry[h], later)
        high = state.astype(BF16)
        low = (state - high.astype(F32)).astype(BF16)
        queries = q[:, cols]
        inter = jnp.dot(queries, high, preferred_element_type=F32)
        inter += jnp.dot(queries, low, preferred_element_type=F32)
        mixed = intra[:, cols] + jnp.exp(run[0, :, h : h + 1]) * inter
        scale = lax.rsqrt(jnp.mean(mixed * mixed, axis=-1, keepdims=True) + 1e-06)
        out[:, cols] = (mixed * scale).astype(BF16)


def params():
    return pltpu.CompilerParams(vmem_limit_bytes=56 * MIB)


def sized(shape, dtype):
    return jax.ShapeDtypeStruct(shape, dtype)


def whole(*shape):
    return pl.BlockSpec(shape, lambda step: (0,) * len(shape))


def slots(matrices):
    return [
        pltpu.VMEM((2, BLK, X * DEPTH), BF16),
        pltpu.VMEM((matrices, X * DEPTH, 4 * HEAD), BF16),
        pltpu.SemaphoreType.DMA((8 + 4 * matrices,)),
    ]


def project_kv(order, tokens, weights, run, last):
    wide = 4 * HEAD
    return pl.pallas_call(
        kv_kernel,
        grid=(1,),
        in_specs=[SCALARS] + [LEFT] * 8 + [whole(2, BLK, 4), whole(2, 4)],
        out_specs=[whole(2 * BLK, wide)] * 2 + [whole(4, HEAD, HEAD)] * 2,
        out_shape=[sized((2 * BLK, wide), BF16)] * 2 + [sized((4, HEAD, HEAD), F32)] * 2,
        scratch_shapes=slots(2),
        compiler_params=params(),
        cost_estimate=pl.CostEstimate(
            flops=4 * BLK * 4096 * 1024, bytes_accessed=20 * MIB, transcendentals=MIB
        ),
        name="keys_values",
    )(order, *tokens, weights, run, last)


def project_q(order, tokens, weights, run, across, k, v):
    wide = 4 * HEAD
    return pl.pallas_call(
        q_kernel,
        grid=(1,),
        in_specs=[SCALARS]
        + [LEFT] * 8
        + [whole(2, BLK, 4), whole(2, 4, BLK)]
        + [whole(2 * BLK, wide)] * 2,
        out_specs=[whole(2 * BLK, wide)] * 2,
        out_shape=[sized((2 * BLK, wide), BF16), sized((2 * BLK, wide), F32)],
        scratch_shapes=slots(1),
        compiler_params=params(),
        cost_estimate=pl.CostEstimate(
            flops=4 * BLK * 4096 * 512, bytes_accessed=20 * MIB, transcendentals=2 * MIB
        ),
        name="queries",
    )(order, *tokens, weights, run, across, k, v)


def finish(q, intra, run, last, entry, fresh):
    block = pl.BlockSpec((BLK, 4 * HEAD), lambda b: (b, 0))
    return pl.pallas_call(
        finish_kernel,
        grid=(2,),
        in_specs=[
            block,
            block,
            pl.BlockSpec((1, BLK, 4), lambda b: (b, 0, 0)),
            whole(2, 4),
            whole(4, HEAD, HEAD),
            whole(4, HEAD, HEAD),
        ],
        out_specs=block,
        out_shape=sized((2 * BLK, 4 * HEAD), BF16),
        compiler_params=params(),
        cost_estimate=pl.CostEstimate(
            flops=8 * BLK * 512 * HEAD, bytes_accessed=5 * MIB, transcendentals=MIB // 64
        ),
        name="finish",
    )(q, intra, run, last, entry, fresh)


def ring(n, by):
    return [(i, (i + by) % n) for i in range(n)]


def gather_tokens(tokens):
    ahead = functools.partial(lax.ppermute, axis_name="fsdp", perm=ring(X, 1))
    back = functools.partial(lax.ppermute, axis_name="fsdp", perm=ring(X, -1))
    top, bottom = tokens[:BLK], tokens[BLK:]
    left0, right1 = ahead(top), back(bottom)
    left1, right0 = ahead(bottom), back(top)
    return left0, right0, ahead(left0), left1, right1, back(right1)


def factors(own, place):
    n = lax.axis_size("seq")
    heads = own.shape[0]
    row = jnp.pad(own, (0, HEAD - heads))
    whole = lax.all_to_all(jnp.broadcast_to(row, (n, 8, HEAD)), "seq", 0, 0, tiled=True)
    at = jnp.arange(n)
    between = (at[None, None, :] > at[None, :, None]) & (at[None, None, :] < at[:, None, None])
    slices = n // heads
    mine = lax.dynamic_index_in_dim(whole[:, 0, :heads], place // slices, 1, False)
    gap = jnp.sum(jnp.where(between, mine[None, None, :], 0.0), axis=2)
    return jnp.where(at[:, None] > at[None, :], jnp.exp(gap), 0.0)


def prefixes(state, factor):
    n = factor.shape[0]
    piece = lax.all_to_all(state.reshape(n, -1, HEAD), "seq", 0, 0, tiled=True)
    return jnp.dot(factor, piece.reshape(n, -1), precision=EXACT).reshape(piece.shape)


def on_device(tokens, projection, log_decay):
    heads = log_decay.shape[1]
    x, place = lax.axis_index("fsdp"), lax.axis_index("seq")
    order = ((x + jnp.array([0, 3, 1, 2])) % X).astype(jnp.int32)

    weights = lax.all_gather(projection, "seq", axis=1, tiled=True)
    moved = gather_tokens(tokens)
    all_tokens = (tokens, *moved)

    decay = log_decay.reshape(2, BLK, heads)
    lower = (jnp.arange(BLK)[:, None] >= jnp.arange(BLK)[None, :]).astype(F32)
    run = jnp.einsum("ts,bsh->bth", lower, decay, precision=EXACT)
    across = run.transpose(0, 2, 1)
    last = run[:, -1]
    factor = factors(last[0] + last[1], place)
    order, run, across, last, weights, factor = lax.optimization_barrier(
        (order, run, across, last, weights, factor)
    )

    k, v, fresh, final = project_kv(order, all_tokens, weights, run, last)
    prefix = prefixes(final, factor)
    q, intra = project_q(order, all_tokens, weights, run, across, k, v)
    entry = lax.all_to_all(prefix, "seq", 0, 0, tiled=True).reshape(final.shape)
    return finish(q, intra, run, last, entry, fresh)


def solution(mesh):
    in_specs = (P("seq", "fsdp"), P(None, "seq", "fsdp"), P("seq", "fsdp"))
    out_specs = P("seq", "fsdp")
    return jax.shard_map(
        on_device, mesh=mesh, in_specs=in_specs, out_specs=out_specs, check_vma=False
    )
```

```python
import functools

import jax
import jax.numpy as jnp
from jax import lax
from jax.experimental import pallas as pl
from jax.experimental.pallas import tpu as pltpu
from jax.sharding import PartitionSpec as P

BLK = 512
HEAD = 128
DEPTH = 1024
X = 4
MIB = 2**20
F32 = jnp.float32
BF16 = jnp.bfloat16
EXACT = lax.Precision.HIGHEST
LEFT = pl.BlockSpec(memory_space=pl.ANY)
SCALARS = pl.BlockSpec(memory_space=pltpu.SMEM)


def silu(v):
    return v / (1.0 + jnp.exp(-v))


class Operands:
    def __init__(self, order, tokens, weights, matrices, token_slots, weight_slots, sems):
        self.token_slots, self.weight_slots = token_slots, weight_slots
        own, *rest = tokens
        self.pending = {}
        count = 0

        def add(key, src, dst):
            nonlocal count
            copy = pltpu.make_async_copy(src, dst, sems.at[count])
            copy.start()
            self.pending.setdefault(key, []).append(copy)
            count += 1

        def token(b):
            for d in range(X):
                src = own.at[pl.ds(b * BLK, BLK)] if d == 0 else rest[3 * b + d - 1]
                add(("t", b), src, token_slots.at[b, :, pl.ds(d * DEPTH, DEPTH)])

        def weight(m):
            for d in range(X):
                rows = pl.ds(pl.multiple_of(order[d] * DEPTH, DEPTH), DEPTH)
                add(("w", m), weights.at[matrices[m], rows], weight_slots.at[m, pl.ds(d * DEPTH, DEPTH)])

        weight(0)
        token(0)
        for m in range(1, len(matrices)):
            weight(m)
        token(1)

    def project(self, b, m):
        for key in (("t", b), ("w", m)):
            for copy in self.pending.pop(key, ()):
                copy.wait()
        return jnp.dot(self.token_slots[b], self.weight_slots[m], preferred_element_type=F32)


def kv_kernel(order, *refs):
    tokens, weights = refs[:7], refs[7]
    run, last, k_out, v_out, fresh, final, *scratch = refs[8:]
    operands = Operands(order, tokens, weights, (1, 2), *scratch)
    for b in range(2):
        rows = slice(b * BLK, (b + 1) * BLK)
        k = silu(operands.project(b, 0)).astype(BF16)
        k_out[rows] = k
        v = operands.project(b, 1).astype(BF16)
        v_out[rows] = v
        for h in range(4):
            cols = slice(h * HEAD, (h + 1) * HEAD)
            ends = last[b : b + 1, h : h + 1]
            fade = jnp.exp(ends - run[b, :, h : h + 1])
            carried = (k[:, cols].astype(F32) * fade).astype(BF16)
            new = lax.dot_general(
                carried, v[:, cols], (((0,), (0,)), ((), ())), preferred_element_type=F32
            )
            if b == 0:
                fresh[h] = new
            else:
                final[h] = (jnp.exp(ends) * fresh[h] + new).astype(BF16)


def q_kernel(order, *refs):
    tokens, weights = refs[:7], refs[7]
    run, across, k, v, q_out, intra, *scratch = refs[8:]
    operands = Operands(order, tokens, weights, (0,), *scratch)
    half = BLK // 2
    for b in range(2):
        base = b * BLK
        q = silu(operands.project(b, 0)).astype(BF16)
        q_out[base : base + BLK] = q
        for h in range(4):
            cols = slice(h * HEAD, (h + 1) * HEAD)
            for t in range(2):
                rows = slice(t * half, (t + 1) * half)
                wide = (t + 1) * half
                scores = lax.dot_general(
                    q[rows, cols],
                    k[base : base + wide, cols],
                    (((1,), (1,)), ((), ())),
                    preferred_element_type=F32,
                )
                gap = run[b, rows, h : h + 1] - across[b, h : h + 1, :wide]
                at = lax.broadcasted_iota(jnp.int32, gap.shape, 0) + t * half
                lower = at >= lax.broadcasted_iota(jnp.int32, gap.shape, 1)
                fading = jnp.exp(jnp.where(lower, gap, -1e30))
                mix = (fading * scores).astype(BF16)
                intra[base + t * half : base + wide, cols] = jnp.dot(
                    mix, v[base : base + wide, cols], preferred_element_type=F32
                )


def finish_kernel(q, intra, run, last, entry, fresh, out):
    b = pl.program_id(0)
    for h in range(4):
        cols = slice(h * HEAD, (h + 1) * HEAD)
        state = entry[h].astype(F32)
        later = jnp.exp(last[0:1, h : h + 1]) * state + fresh[h]
        state = jnp.where(b == 0, state, later).astype(BF16)
        inter = jnp.dot(q[:, cols], state, preferred_element_type=F32)
        mixed = intra[:, cols] + jnp.exp(run[0, :, h : h + 1]) * inter
        scale = lax.rsqrt(jnp.mean(mixed * mixed, axis=-1, keepdims=True) + 1e-06)
        out[:, cols] = (mixed * scale).astype(BF16)


def params():
    return pltpu.CompilerParams(vmem_limit_bytes=56 * MIB)


def sized(shape, dtype):
    return jax.ShapeDtypeStruct(shape, dtype)


def whole(*shape):
    return pl.BlockSpec(shape, lambda step: (0,) * len(shape))


def slots(matrices):
    return [
        pltpu.VMEM((2, BLK, X * DEPTH), BF16),
        pltpu.VMEM((matrices, X * DEPTH, 4 * HEAD), BF16),
        pltpu.SemaphoreType.DMA((8 + 4 * matrices,)),
    ]


def project_kv(order, tokens, weights, run, last):
    wide = 4 * HEAD
    return pl.pallas_call(
        kv_kernel,
        grid=(1,),
        in_specs=[SCALARS] + [LEFT] * 8 + [whole(2, BLK, 4), whole(2, 4)],
        out_specs=[whole(2 * BLK, wide)] * 2 + [whole(4, HEAD, HEAD)] * 2,
        out_shape=[sized((2 * BLK, wide), BF16)] * 2
        + [sized((4, HEAD, HEAD), F32), sized((4, HEAD, HEAD), BF16)],
        scratch_shapes=slots(2),
        compiler_params=params(),
        cost_estimate=pl.CostEstimate(
            flops=4 * BLK * 4096 * 1024, bytes_accessed=20 * MIB, transcendentals=MIB
        ),
        name="keys_values",
    )(order, *tokens, weights, run, last)


def project_q(order, tokens, weights, run, across, k, v):
    wide = 4 * HEAD
    return pl.pallas_call(
        q_kernel,
        grid=(1,),
        in_specs=[SCALARS]
        + [LEFT] * 8
        + [whole(2, BLK, 4), whole(2, 4, BLK)]
        + [whole(2 * BLK, wide)] * 2,
        out_specs=[whole(2 * BLK, wide)] * 2,
        out_shape=[sized((2 * BLK, wide), BF16), sized((2 * BLK, wide), F32)],
        scratch_shapes=slots(1),
        compiler_params=params(),
        cost_estimate=pl.CostEstimate(
            flops=4 * BLK * 4096 * 512, bytes_accessed=20 * MIB, transcendentals=2 * MIB
        ),
        name="queries",
    )(order, *tokens, weights, run, across, k, v)


def finish(q, intra, run, last, entry, fresh):
    block = pl.BlockSpec((BLK, 4 * HEAD), lambda b: (b, 0))
    return pl.pallas_call(
        finish_kernel,
        grid=(2,),
        in_specs=[
            block,
            block,
            pl.BlockSpec((1, BLK, 4), lambda b: (b, 0, 0)),
            whole(2, 4),
            whole(4, HEAD, HEAD),
            whole(4, HEAD, HEAD),
        ],
        out_specs=block,
        out_shape=sized((2 * BLK, 4 * HEAD), BF16),
        compiler_params=params(),
        cost_estimate=pl.CostEstimate(
            flops=8 * BLK * 512 * HEAD, bytes_accessed=5 * MIB, transcendentals=MIB // 64
        ),
        name="finish",
    )(q, intra, run, last, entry, fresh)


def ring(n, by):
    return [(i, (i + by) % n) for i in range(n)]


def gather_tokens(tokens):
    ahead = functools.partial(lax.ppermute, axis_name="fsdp", perm=ring(X, 1))
    back = functools.partial(lax.ppermute, axis_name="fsdp", perm=ring(X, -1))
    top, bottom = tokens[:BLK], tokens[BLK:]
    left0, right1 = ahead(top), back(bottom)
    left1, right0 = ahead(bottom), back(top)
    return left0, right0, ahead(left0), left1, right1, back(right1)


def factors(own, place):
    n = lax.axis_size("seq")
    heads = own.shape[0]
    row = jnp.pad(own, (0, HEAD - heads))
    whole = lax.all_to_all(jnp.broadcast_to(row, (n, 8, HEAD)), "seq", 0, 0, tiled=True)
    at = jnp.arange(n)
    between = (at[None, None, :] > at[None, :, None]) & (at[None, None, :] < at[:, None, None])
    slices = n // heads
    mine = lax.dynamic_index_in_dim(whole[:, 0, :heads], place // slices, 1, False)
    gap = jnp.sum(jnp.where(between, mine[None, None, :], 0.0), axis=2)
    return jnp.where(at[:, None] > at[None, :], jnp.exp(gap), 0.0)


def prefixes(state, factor):
    n = factor.shape[0]
    piece = lax.all_to_all(state.reshape(n, -1, HEAD), "seq", 0, 0, tiled=True)
    prefix = jnp.dot(factor, piece.astype(F32).reshape(n, -1), precision=EXACT)
    return prefix.astype(BF16).reshape(piece.shape)


def on_device(tokens, projection, log_decay):
    heads = log_decay.shape[1]
    x, place = lax.axis_index("fsdp"), lax.axis_index("seq")
    order = ((x + jnp.array([0, 3, 1, 2])) % X).astype(jnp.int32)

    weights = lax.all_gather(projection, "seq", axis=1, tiled=True)
    moved = gather_tokens(tokens)
    all_tokens = (tokens, *moved)

    decay = log_decay.reshape(2, BLK, heads)
    lower = (jnp.arange(BLK)[:, None] >= jnp.arange(BLK)[None, :]).astype(F32)
    run = jnp.einsum("ts,bsh->bth", lower, decay, precision=EXACT)
    across = run.transpose(0, 2, 1)
    last = run[:, -1]
    factor = factors(last[0] + last[1], place)
    order, run, across, last, weights, factor = lax.optimization_barrier(
        (order, run, across, last, weights, factor)
    )

    k, v, fresh, final = project_kv(order, all_tokens, weights, run, last)
    prefix = prefixes(final, factor)
    q, intra = project_q(order, all_tokens, weights, run, across, k, v)
    entry = lax.all_to_all(prefix, "seq", 0, 0, tiled=True).reshape(final.shape)
    return finish(q, intra, run, last, entry, fresh)


def solution(mesh):
    in_specs = (P("seq", "fsdp"), P(None, "seq", "fsdp"), P("seq", "fsdp"))
    out_specs = P("seq", "fsdp")
    return jax.shard_map(
        on_device, mesh=mesh, in_specs=in_specs, out_specs=out_specs, check_vma=False
    )
```

```python
import functools

import jax
import jax.numpy as jnp
from jax import lax
from jax.experimental import pallas as pl
from jax.experimental.pallas import tpu as pltpu
from jax.sharding import PartitionSpec as P

BLK = 512
HEAD = 128
DEPTH = 1024
X = 4
MIB = 2**20
F32 = jnp.float32
BF16 = jnp.bfloat16
EXACT = lax.Precision.HIGHEST
LEFT = pl.BlockSpec(memory_space=pl.ANY)
SCALARS = pl.BlockSpec(memory_space=pltpu.SMEM)


def silu(v):
    return v / (1.0 + jnp.exp(-v))


class Operands:
    def __init__(self, order, tokens, weights, matrices, token_slots, weight_slots, sems):
        self.token_slots, self.weight_slots = token_slots, weight_slots
        own, *rest = tokens
        self.pending = {}
        count = 0

        def add(key, src, dst):
            nonlocal count
            copy = pltpu.make_async_copy(src, dst, sems.at[count])
            copy.start()
            self.pending.setdefault(key, []).append(copy)
            count += 1

        def token(b):
            for d in range(X):
                src = own.at[pl.ds(b * BLK, BLK)] if d == 0 else rest[3 * b + d - 1]
                add(("t", b), src, token_slots.at[b, :, pl.ds(d * DEPTH, DEPTH)])

        def weight(m):
            for d in range(X):
                rows = pl.ds(pl.multiple_of(order[d] * DEPTH, DEPTH), DEPTH)
                add(("w", m), weights.at[matrices[m], rows], weight_slots.at[m, pl.ds(d * DEPTH, DEPTH)])

        weight(0)
        token(0)
        for m in range(1, len(matrices)):
            weight(m)
        token(1)

    def project(self, b, m):
        for key in (("t", b), ("w", m)):
            for copy in self.pending.pop(key, ()):
                copy.wait()
        return jnp.dot(self.token_slots[b], self.weight_slots[m], preferred_element_type=F32)


def kv_kernel(order, *refs):
    tokens, weights = refs[:7], refs[7]
    run, last, k_out, v_out, fresh, final, *scratch = refs[8:]
    operands = Operands(order, tokens, weights, (1, 2), *scratch)
    for b in range(2):
        rows = slice(b * BLK, (b + 1) * BLK)
        k = silu(operands.project(b, 0)).astype(BF16)
        k_out[rows] = k
        v = operands.project(b, 1).astype(BF16)
        v_out[rows] = v
        for h in range(4):
            cols = slice(h * HEAD, (h + 1) * HEAD)
            ends = last[b : b + 1, h : h + 1]
            fade = jnp.exp(ends - run[b, :, h : h + 1])
            carried = (k[:, cols].astype(F32) * fade).astype(BF16)
            new = lax.dot_general(
                carried, v[:, cols], (((0,), (0,)), ((), ())), preferred_element_type=F32
            )
            if b == 0:
                fresh[h] = new
            else:
                final[h] = (jnp.exp(ends) * fresh[h] + new).astype(BF16)


def q_kernel(order, *refs):
    tokens, weights = refs[:7], refs[7]
    run, across, k, v, q_out, intra, *scratch = refs[8:]
    operands = Operands(order, tokens, weights, (0,), *scratch)
    half = BLK // 2
    for b in range(2):
        base = b * BLK
        q = silu(operands.project(b, 0)).astype(BF16)
        q_out[base : base + BLK] = q
        for h in range(4):
            cols = slice(h * HEAD, (h + 1) * HEAD)
            for t in range(2):
                rows = slice(t * half, (t + 1) * half)
                total = None
                for u in range(t + 1):
                    seen = slice(base + u * half, base + (u + 1) * half)
                    scores = lax.dot_general(
                        q[rows, cols],
                        k[seen, cols],
                        (((1,), (1,)), ((), ())),
                        preferred_element_type=F32,
                    )
                    gap = run[b, rows, h : h + 1] - across[b, h : h + 1, u * half : (u + 1) * half]
                    if u == t:
                        at = lax.broadcasted_iota(jnp.int32, gap.shape, 0)
                        lower = at >= lax.broadcasted_iota(jnp.int32, gap.shape, 1)
                        gap = jnp.where(lower, gap, -1e30)
                    mix = (jnp.exp(gap) * scores).astype(BF16)
                    part = jnp.dot(mix, v[seen, cols], preferred_element_type=F32)
                    total = part if u == 0 else total + part
                intra[base + t * half : base + (t + 1) * half, cols] = total


def finish_kernel(q, intra, run, last, entry, fresh, out):
    b = pl.program_id(0)
    for h in range(4):
        cols = slice(h * HEAD, (h + 1) * HEAD)
        state = entry[h].astype(F32)
        later = jnp.exp(last[0:1, h : h + 1]) * state + fresh[h]
        state = jnp.where(b == 0, state, later).astype(BF16)
        inter = jnp.dot(q[:, cols], state, preferred_element_type=F32)
        mixed = intra[:, cols] + jnp.exp(run[0, :, h : h + 1]) * inter
        scale = lax.rsqrt(jnp.mean(mixed * mixed, axis=-1, keepdims=True) + 1e-06)
        out[:, cols] = (mixed * scale).astype(BF16)


def params():
    return pltpu.CompilerParams(vmem_limit_bytes=56 * MIB)


def sized(shape, dtype):
    return jax.ShapeDtypeStruct(shape, dtype)


def whole(*shape):
    return pl.BlockSpec(shape, lambda step: (0,) * len(shape))


def slots(matrices):
    return [
        pltpu.VMEM((2, BLK, X * DEPTH), BF16),
        pltpu.VMEM((matrices, X * DEPTH, 4 * HEAD), BF16),
        pltpu.SemaphoreType.DMA((8 + 4 * matrices,)),
    ]


def project_kv(order, tokens, weights, run, last):
    wide = 4 * HEAD
    return pl.pallas_call(
        kv_kernel,
        grid=(1,),
        in_specs=[SCALARS] + [LEFT] * 8 + [whole(2, BLK, 4), whole(2, 4)],
        out_specs=[whole(2 * BLK, wide)] * 2 + [whole(4, HEAD, HEAD)] * 2,
        out_shape=[sized((2 * BLK, wide), BF16)] * 2
        + [sized((4, HEAD, HEAD), F32), sized((4, HEAD, HEAD), BF16)],
        scratch_shapes=slots(2),
        compiler_params=params(),
        cost_estimate=pl.CostEstimate(
            flops=4 * BLK * 4096 * 1024, bytes_accessed=20 * MIB, transcendentals=MIB
        ),
        name="keys_values",
    )(order, *tokens, weights, run, last)


def project_q(order, tokens, weights, run, across, k, v):
    wide = 4 * HEAD
    return pl.pallas_call(
        q_kernel,
        grid=(1,),
        in_specs=[SCALARS]
        + [LEFT] * 8
        + [whole(2, BLK, 4), whole(2, 4, BLK)]
        + [whole(2 * BLK, wide)] * 2,
        out_specs=[whole(2 * BLK, wide)] * 2,
        out_shape=[sized((2 * BLK, wide), BF16), sized((2 * BLK, wide), F32)],
        scratch_shapes=slots(1),
        compiler_params=params(),
        cost_estimate=pl.CostEstimate(
            flops=4 * BLK * 4096 * 512, bytes_accessed=20 * MIB, transcendentals=2 * MIB
        ),
        name="queries",
    )(order, *tokens, weights, run, across, k, v)


def finish(q, intra, run, last, entry, fresh):
    block = pl.BlockSpec((BLK, 4 * HEAD), lambda b: (b, 0))
    return pl.pallas_call(
        finish_kernel,
        grid=(2,),
        in_specs=[
            block,
            block,
            pl.BlockSpec((1, BLK, 4), lambda b: (b, 0, 0)),
            whole(2, 4),
            whole(4, HEAD, HEAD),
            whole(4, HEAD, HEAD),
        ],
        out_specs=block,
        out_shape=sized((2 * BLK, 4 * HEAD), BF16),
        compiler_params=params(),
        cost_estimate=pl.CostEstimate(
            flops=8 * BLK * 512 * HEAD, bytes_accessed=5 * MIB, transcendentals=MIB // 64
        ),
        name="finish",
    )(q, intra, run, last, entry, fresh)


def ring(n, by):
    return [(i, (i + by) % n) for i in range(n)]


def gather_tokens(tokens):
    ahead = functools.partial(lax.ppermute, axis_name="fsdp", perm=ring(X, 1))
    back = functools.partial(lax.ppermute, axis_name="fsdp", perm=ring(X, -1))
    top, bottom = tokens[:BLK], tokens[BLK:]
    left0, right1 = ahead(top), back(bottom)
    left1, right0 = ahead(bottom), back(top)
    return left0, right0, ahead(left0), left1, right1, back(right1)


def factors(own, place):
    n = lax.axis_size("seq")
    heads = own.shape[0]
    row = jnp.pad(own, (0, HEAD - heads))
    whole = lax.all_to_all(jnp.broadcast_to(row, (n, 8, HEAD)), "seq", 0, 0, tiled=True)
    at = jnp.arange(n)
    between = (at[None, None, :] > at[None, :, None]) & (at[None, None, :] < at[:, None, None])
    slices = n // heads
    mine = lax.dynamic_index_in_dim(whole[:, 0, :heads], place // slices, 1, False)
    gap = jnp.sum(jnp.where(between, mine[None, None, :], 0.0), axis=2)
    return jnp.where(at[:, None] > at[None, :], jnp.exp(gap), 0.0)


def prefixes(state, factor):
    n = factor.shape[0]
    piece = lax.all_to_all(state.reshape(n, -1, HEAD), "seq", 0, 0, tiled=True)
    prefix = jnp.dot(factor, piece.astype(F32).reshape(n, -1), precision=EXACT)
    return prefix.astype(BF16).reshape(piece.shape)


def on_device(tokens, projection, log_decay):
    heads = log_decay.shape[1]
    x, place = lax.axis_index("fsdp"), lax.axis_index("seq")
    order = ((x + jnp.array([0, 3, 1, 2])) % X).astype(jnp.int32)

    weights = lax.all_gather(projection, "seq", axis=1, tiled=True)
    moved = gather_tokens(tokens)
    all_tokens = (tokens, *moved)

    decay = log_decay.reshape(2, BLK, heads)
    lower = (jnp.arange(BLK)[:, None] >= jnp.arange(BLK)[None, :]).astype(F32)
    run = jnp.einsum("ts,bsh->bth", lower, decay, precision=EXACT)
    across = run.transpose(0, 2, 1)
    last = run[:, -1]
    factor = factors(last[0] + last[1], place)
    order, run, across, last, weights, factor = lax.optimization_barrier(
        (order, run, across, last, weights, factor)
    )

    k, v, fresh, final = project_kv(order, all_tokens, weights, run, last)
    prefix = prefixes(final, factor)
    q, intra = project_q(order, all_tokens, weights, run, across, k, v)
    entry = lax.all_to_all(prefix, "seq", 0, 0, tiled=True).reshape(final.shape)
    return finish(q, intra, run, last, entry, fresh)


def solution(mesh):
    in_specs = (P("seq", "fsdp"), P(None, "seq", "fsdp"), P("seq", "fsdp"))
    out_specs = P("seq", "fsdp")
    return jax.shard_map(
        on_device, mesh=mesh, in_specs=in_specs, out_specs=out_specs, check_vma=False
    )
```
